32 devices in a mesh: ctx: 16 (over z, x, core), head: 2 (over y).
Axes of the slice: x: 2, y: 2, z: 4, core: 2. Of those that a mesh axis runs over, the one named last changes fastest.
Arguments:
- queries: bfloat16 [4096, 8192], P('ctx', 'head'), may hold values from -5 to 5
- keys: bfloat16 [4096, 512], P(('ctx', 'head')), may hold values from -5 to 5
- values: bfloat16 [4096, 512], P(('ctx', 'head')), may hold values from -6 to 6
- d_out: bfloat16 [4096, 8192], P('ctx', 'head'), may hold values from -6 to 6
- selected: int32 [64, 12], P('ctx'), may hold values from 0 to 11, as said below
- partners: int32 [2, 16], replicated, may hold values from 0 to 15, as said below
Outputs:
- attended: bfloat16 [4096, 8192], P('ctx', 'head')
- grad_queries: bfloat16 [4096, 8192], P('ctx', 'head')
- grad_keys: bfloat16 [4096, 512], P(('ctx', 'head'))
- grad_values: bfloat16 [4096, 512], P(('ctx', 'head'))
The draws below stay inside these ranges and needn't reach their ends.
Inputs may be any that keep to these rules, and one draw needn't show every extreme that they name: `selected`: row b lists 12 different candidate blocks of query block b: 0 to 3 are its own shard's key blocks, 4 to 7 those of its partner under the first matching, 8 to 11 those under the second; the first entry is the query block's own key block (b modulo 4). `partners`: row r gives for every shard i its partner i XOR m_r, with a mask m_r that is the same for all shards; one of the two masks is 8, the other is 2 ** j - 1 for some j of 1 to 4, and either may stand in either row.
All inputs are finite; a program needn't handle non-finite values.
Results may differ from the reference program's by a relative error of at most 0.018.
Values may be sent and summed in bfloat16 or wider, within the bound.
A program may use at most 128 MiB of HBM per device.

```python
import jax
import jax.numpy as jnp
from jax import lax

HQ = 64
KVH = 4
DH = 128
BLK = 64
SEL = 12
TOK_DEV = 256
SHARDS = 16
LOGC = 4
TOKENS = 4096
NQB = 64


def draw_queries(key, part):
    full_shape = (TOKENS, HQ * DH)
    return jnp.clip(jax.random.normal(jax.random.fold_in(key, 1), full_shape, jnp.float32), -5.0, 5.0).astype(jnp.bfloat16)


def draw_keys(key, part):
    full_shape = (TOKENS, KVH * DH)
    return jnp.clip(jax.random.normal(jax.random.fold_in(key, 2), full_shape, jnp.float32), -5.0, 5.0).astype(jnp.bfloat16)


def draw_selected(key, part):
    block_count = TOK_DEV // BLK
    cand_total = 3 * block_count
    own_block = (jnp.arange(NQB, dtype=jnp.int32) % block_count).astype(jnp.int32)
    row_keys = jax.random.split(jax.random.fold_in(key, 3), NQB)
    picked = jax.vmap(lambda row_key: jax.random.permutation(row_key, cand_total - 1)[:SEL - 1])(row_keys).astype(jnp.int32)
    others = picked + (picked >= own_block[:, None]).astype(jnp.int32)
    return jnp.concatenate([own_block[:, None], others], axis=1).astype(jnp.int32)


def draw_partners(key, part):
    half_mask = jnp.array(SHARDS // 2, jnp.int32)
    low_bits = jax.random.randint(jax.random.fold_in(key, 4), (), 1, LOGC + 1, jnp.int32)
    low_mask = (jnp.left_shift(jnp.array(1, jnp.int32), low_bits) - 1).astype(jnp.int32)
    flip = jax.random.randint(jax.random.fold_in(key, 5), (), 0, 2, jnp.int32)
    first_mask = jnp.where(flip == 1, half_mask, low_mask).astype(jnp.int32)
    second_mask = jnp.where(flip == 1, low_mask, half_mask).astype(jnp.int32)
    shard_ids = jnp.arange(SHARDS, dtype=jnp.int32)
    return jnp.stack([jnp.bitwise_xor(shard_ids, first_mask), jnp.bitwise_xor(shard_ids, second_mask)]).astype(jnp.int32)


def block_levels(own_key, shape, shards, smallest, high):
    gain = 1.0
    for axis_at, shards_of in shards:
        heights = jax.random.uniform(jax.random.fold_in(jax.random.fold_in(own_key, 6), axis_at), (shards_of,), jnp.float32, smallest / len(shards), high / len(shards))
        gain = gain * jnp.repeat(jnp.exp(heights), shape[axis_at] // shards_of).reshape((-1,) + (1,) * (len(shape) - 1 - axis_at))
    return gain


def centred(stream_key, dims, deviation, most, pieces=(), kind=jnp.bfloat16):
    loudness = block_levels(stream_key, dims, pieces, -0.22, 0.18) if pieces else 1.0
    values = jax.random.normal(stream_key, dims, jnp.float32) * deviation * loudness
    return jnp.minimum(jnp.maximum(values, -most), most).astype(kind)


def setup_inputs(seed: int = 0) -> dict:
    key_of = jax.random.split(jax.random.key(seed), 7)
    queries = draw_queries(jax.random.fold_in(key_of[6], 71), 0)
    keys = draw_keys(jax.random.fold_in(key_of[6], 71), 0)
    values = centred(key_of[2], (TOKENS, KVH * DH), 1.0, 6.0, ((0, 32),))
    d_out = centred(key_of[3], (TOKENS, HQ * DH), 1.0, 6.0, ((0, 16), (1, 2)))
    selected = draw_selected(jax.random.fold_in(key_of[6], 71), 0)
    partners = draw_partners(jax.random.fold_in(key_of[6], 71), 0)
    return dict(queries=queries, keys=keys, values=values, d_out=d_out, selected=selected, partners=partners)


def rounded(values_in):
    return lax.optimization_barrier(values_in.astype(jnp.bfloat16)).astype(jnp.float32)


def attend_shard(query_rows, cand_keys, cand_values, grad_rows, chosen_rows):
    block_count = TOK_DEV // BLK
    group_size = HQ // KVH
    score_scale = DH ** -0.5
    key_blocks = cand_keys.astype(jnp.float32).reshape(3 * block_count, BLK, KVH, DH)
    value_blocks = cand_values.astype(jnp.float32).reshape(3 * block_count, BLK, KVH, DH)
    key_terms = jnp.zeros((3 * block_count, BLK, KVH, DH), jnp.float32)
    value_terms = jnp.zeros((3 * block_count, BLK, KVH, DH), jnp.float32)
    out_parts = []
    grad_parts = []
    for block_index in range(block_count):
        row_lo = block_index * BLK
        query_block = query_rows[row_lo:row_lo + BLK].astype(jnp.float32).reshape(BLK, KVH, group_size, DH)
        grad_block = grad_rows[row_lo:row_lo + BLK].astype(jnp.float32).reshape(BLK, KVH, group_size, DH)
        chosen = chosen_rows[block_index]
        picked_keys = key_blocks[chosen].reshape(SEL * BLK, KVH, DH)
        picked_values = value_blocks[chosen].reshape(SEL * BLK, KVH, DH)
        scores = jnp.einsum("qgrd,kgd->grqk", query_block, picked_keys) * score_scale
        prob_full = jax.nn.softmax(scores, axis=-1)
        prob_low = rounded(prob_full)
        out_block = rounded(jnp.einsum("grqk,kgd->qgrd", prob_low, picked_values))
        grad_p = jnp.einsum("qgrd,kgd->grqk", grad_block, picked_values)
        row_delta = jnp.einsum("qgrd,qgrd->grq", grad_block, out_block)
        grad_s = rounded(prob_full * (grad_p - row_delta[..., None]) * score_scale)
        grad_q = rounded(jnp.einsum("grqk,kgd->qgrd", grad_s, picked_keys))
        key_part = jnp.einsum("grqk,qgrd->kgd", grad_s, query_block).reshape(SEL, BLK, KVH, DH)
        value_part = jnp.einsum("grqk,qgrd->kgd", prob_low, grad_block).reshape(SEL, BLK, KVH, DH)
        key_terms = key_terms.at[chosen].add(key_part)
        value_terms = value_terms.at[chosen].add(value_part)
        out_parts.append(out_block.reshape(BLK, HQ * DH))
        grad_parts.append(grad_q.reshape(BLK, HQ * DH))
    attended = jnp.concatenate(out_parts, 0).astype(jnp.bfloat16)
    grad_queries = jnp.concatenate(grad_parts, 0).astype(jnp.bfloat16)
    return (attended, grad_queries, key_terms.reshape(3 * TOK_DEV, KVH * DH), value_terms.reshape(3 * TOK_DEV, KVH * DH))


def reference(queries, keys, values, d_out, selected, partners):
    block_count = TOK_DEV // BLK
    query_shards = queries.reshape(SHARDS, TOK_DEV, HQ * DH)
    grad_shards = d_out.reshape(SHARDS, TOK_DEV, HQ * DH)
    key_shards = keys.reshape(SHARDS, TOK_DEV, KVH * DH)
    value_shards = values.reshape(SHARDS, TOK_DEV, KVH * DH)
    chosen_shards = selected.reshape(SHARDS, block_count, SEL)

    def one_shard(shard):
        first = partners[0, shard]
        second = partners[1, shard]
        cand_keys = jnp.concatenate([key_shards[shard], key_shards[first], key_shards[second]], 0)
        cand_values = jnp.concatenate([value_shards[shard], value_shards[first], value_shards[second]], 0)
        return attend_shard(query_shards[shard], cand_keys, cand_values, grad_shards[shard], chosen_shards[shard])

    attended, grad_queries, key_terms, value_terms = lax.map(one_shard, jnp.arange(SHARDS, dtype=jnp.int32))

    def combine(terms):
        own_part = terms[:, :TOK_DEV]
        from_first = rounded(terms[:, TOK_DEV:2 * TOK_DEV])
        from_second = rounded(terms[:, 2 * TOK_DEV:])
        total = own_part + from_first[partners[0]] + from_second[partners[1]]
        return total.astype(jnp.bfloat16).reshape(TOKENS, KVH * DH)

    return (attended.reshape(TOKENS, HQ * DH), grad_queries.reshape(TOKENS, HQ * DH), combine(key_terms), combine(value_terms))
```

```python
import functools

import jax
import jax.numpy as jnp
from jax import lax
from jax.experimental import pallas as pl
from jax.experimental.pallas import tpu as pltpu
from jax.sharding import PartitionSpec as P

HQ = 64
KVH = 4
DH = 128
BLK = 64
SEL = 12
PAIR = 2
SCALE = DH**-0.5
LOG2E = 1.4426950408889634
MESH = pl.DeviceIdType.MESH


def nt_dot(left, right):
    return lax.dot_general(
        left, right, (((1,), (1,)), ((), ())), preferred_element_type=jnp.float32
    )


def nn_dot(left, right):
    return jnp.dot(left, right, preferred_element_type=jnp.float32)


def one_head(q, g, k, v, kt, vt):
    qt = q.T
    gt = g.T
    scores = nn_dot(k, qt)
    grad_p = nn_dot(v, gt)
    top = jnp.max(scores, axis=0, keepdims=True)
    e = jnp.exp2((scores - top) * (SCALE * LOG2E))
    inv = 1.0 / jnp.sum(e, axis=0, keepdims=True)
    e_low = e.astype(jnp.bfloat16)
    ot = (nn_dot(vt, e_low) * inv).astype(jnp.bfloat16)
    gt32 = gt.astype(jnp.float32)
    delta = jnp.sum(gt32 * ot.astype(jnp.float32), axis=0, keepdims=True)
    ds = (e * (grad_p - delta)).astype(jnp.bfloat16)
    inv_s = inv * SCALE
    dqt = (nn_dot(kt, ds) * inv_s).astype(jnp.bfloat16)
    q_n = (qt.astype(jnp.float32) * inv_s).astype(jnp.bfloat16)
    g_n = (gt32 * inv).astype(jnp.bfloat16)
    return ot.T, dqt.T, nt_dot(ds, q_n), nt_dot(e_low, g_n)


def attend_kernel(steps, q_ref, g_ref, k_ref, v_ref, o_ref, dq_ref, dk_ref, dv_ref,
                  kt_ref, vt_ref, dk_acc, dv_acc):
    step = pl.program_id(1)

    @pl.when(step == 0)
    def _():
        kt_ref[...] = k_ref[...].T
        vt_ref[...] = v_ref[...].T
        dk_acc[...] = jnp.zeros_like(dk_acc)
        dv_acc[...] = jnp.zeros_like(dv_acc)

    k, v, kt, vt = k_ref[...], v_ref[...], kt_ref[...], vt_ref[...]
    dk_sum = dv_sum = None
    for i in range(PAIR):
        cols = slice(i * DH, (i + 1) * DH)
        o, dq, dk, dv = one_head(q_ref[:, cols], g_ref[:, cols], k, v, kt, vt)
        o_ref[:, cols] = o
        dq_ref[:, cols] = dq
        dk_sum = dk if dk_sum is None else dk_sum + dk
        dv_sum = dv if dv_sum is None else dv_sum + dv
    dk_acc[...] += dk_sum
    dv_acc[...] += dv_sum

    @pl.when(step == steps - 1)
    def _():
        dk_ref[...] = dk_acc[...].astype(jnp.bfloat16)
        dv_ref[...] = dv_acc[...].astype(jnp.bfloat16)


def attend(queries, d_out, keys, values):
    tokens, width = queries.shape
    cand, kv_width = keys.shape
    groups = kv_width // DH
    heads = width // DH // groups
    steps = heads // PAIR
    row_spec = pl.BlockSpec((tokens, PAIR * DH), lambda g, s: (0, g * steps + s))
    kv_spec = pl.BlockSpec((cand, DH), lambda g, s: (0, g))
    elems = tokens * cand * heads * groups
    return pl.pallas_call(
        functools.partial(attend_kernel, steps),
        grid=(groups, steps),
        in_specs=[row_spec, row_spec, kv_spec, kv_spec],
        out_specs=[row_spec, row_spec, kv_spec, kv_spec],
        out_shape=[
            jax.ShapeDtypeStruct(queries.shape, jnp.bfloat16),
            jax.ShapeDtypeStruct(queries.shape, jnp.bfloat16),
            jax.ShapeDtypeStruct(keys.shape, jnp.bfloat16),
            jax.ShapeDtypeStruct(keys.shape, jnp.bfloat16),
        ],
        scratch_shapes=[
            pltpu.VMEM((DH, cand), jnp.bfloat16),
            pltpu.VMEM((DH, cand), jnp.bfloat16),
            pltpu.VMEM((cand, DH), jnp.float32),
            pltpu.VMEM((cand, DH), jnp.float32),
        ],
        compiler_params=pltpu.CompilerParams(vmem_limit_bytes=48 * 2**20),
        cost_estimate=pl.CostEstimate(
            flops=12 * elems * DH, bytes_accessed=8 * tokens * width, transcendentals=elems
        ),
    )(queries, d_out, keys, values)


def partner_shards(low, shards):
    me = lax.axis_index("ctx")
    part = lax.rem(me, low + 1)
    return (me, lax.rem(me + shards // 2, shards), me - part + (low - part))


def peers(low, shards, heads):
    head = lax.axis_index("head")
    found = []
    for slot, shard in enumerate(partner_shards(low, shards)):
        for turn in range(heads):
            if slot or turn:
                found.append((slot, turn, shard, lax.rem(head + turn, heads)))
    return found


def greet(found):
    barrier = pltpu.get_barrier_semaphore()
    for slot, turn, shard, head in found:
        pl.semaphore_signal(barrier, inc=1, device_id=(shard, head), device_id_type=MESH)
    pl.semaphore_wait(barrier, len(found))


def fetch_kernel(low, shards, heads, k_ref, v_ref, kc_ref, vc_ref, send_sem, recv_sem, own_sem):
    me = lax.axis_index("head")
    rows = k_ref.shape[0]
    width = kc_ref.shape[1]
    found = peers(low, shards, heads)
    greet(found)
    copies = []
    pairs = ((k_ref, kc_ref), (v_ref, vc_ref))
    for slot, turn, shard, head in sorted(found, key=lambda f: (f[0] != 1, f[0] != 2)):
        for which, (src, dst) in enumerate(pairs):
            copies.append(
                pltpu.make_async_remote_copy(
                    src_ref=src.at[:, pl.ds(pl.multiple_of(head * width, width), width)],
                    dst_ref=dst.at[
                        pl.ds(pl.multiple_of(slot * rows * heads + me * rows, rows), rows), :
                    ],
                    send_sem=send_sem.at[which, slot, turn],
                    recv_sem=recv_sem.at[which, slot, turn],
                    device_id=(shard, head),
                    device_id_type=MESH,
                )
            )
    for which, (src, dst) in enumerate(pairs):
        copies.append(
            pltpu.make_async_copy(
                src.at[:, pl.ds(pl.multiple_of(me * width, width), width)],
                dst.at[pl.ds(pl.multiple_of(me * rows, rows), rows), :],
                own_sem.at[which],
            )
        )
    for copy in copies:
        copy.start()
    for copy in copies:
        copy.wait()


def return_kernel(low, shards, heads, kt_ref, vt_ref, gk_ref, gv_ref, kr, vr, send_sem, recv_sem,
                  own_sem):
    me = lax.axis_index("head")
    rows = gk_ref.shape[0]
    width = kt_ref.shape[1]
    found = peers(low, shards, heads)
    greet(found)
    copies = []
    pairs = ((kt_ref, kr), (vt_ref, vr))
    for slot, turn, shard, head in sorted(found, key=lambda f: (f[0] != 1, f[0] != 2)):
        for which, (src, dst) in enumerate(pairs):
            copies.append(
                pltpu.make_async_remote_copy(
                    src_ref=src.at[
                        pl.ds(pl.multiple_of(slot * rows * heads + head * rows, rows), rows), :
                    ],
                    dst_ref=dst.at[slot, :, pl.ds(pl.multiple_of(me * width, width), width)],
                    send_sem=send_sem.at[which, slot, turn],
                    recv_sem=recv_sem.at[which, slot, turn],
                    device_id=(shard, head),
                    device_id_type=MESH,
                )
            )
    for which, (src, dst) in enumerate(pairs):
        copies.append(
            pltpu.make_async_copy(
                src.at[pl.ds(pl.multiple_of(me * rows, rows), rows), :],
                dst.at[0, :, pl.ds(pl.multiple_of(me * width, width), width)],
                own_sem.at[which],
            )
        )
    for copy in copies:
        copy.start()
    for copy in copies:
        copy.wait()
    for out, got in ((gk_ref, kr), (gv_ref, vr)):
        total = got[0].astype(jnp.float32)
        for slot in (1, 2):
            total = total + got[slot].astype(jnp.float32)
        out[...] = total.astype(jnp.bfloat16)


def exchange(kernel, first_id, index, low, shards, heads, scratch, out_shape, *operands):
    return pl.pallas_call(
        functools.partial(kernel, low, shards, heads),
        in_specs=[pl.BlockSpec(memory_space=pltpu.VMEM)] * 2,
        out_specs=[pl.BlockSpec(memory_space=pltpu.VMEM)] * 2,
        out_shape=[jax.ShapeDtypeStruct(out_shape, jnp.bfloat16)] * 2,
        scratch_shapes=scratch
        + [
            pltpu.SemaphoreType.DMA((2, 3, heads)),
            pltpu.SemaphoreType.DMA((2, 3, heads)),
            pltpu.SemaphoreType.DMA((2,)),
        ],
        compiler_params=pltpu.CompilerParams(
            collective_id=first_id + index,
            has_side_effects=True,
            vmem_limit_bytes=32 * 2**20,
        ),
    )(*operands)


def body(queries, keys, values, d_out, selected, partners):
    shards = lax.axis_size("ctx")
    heads = lax.axis_size("head")
    bits = shards.bit_length() - 1
    rows = keys.shape[0]
    tokens = rows * heads
    width = keys.shape[1] // heads
    assert selected.shape[1] == 3 * tokens // BLK
    half = shards // 2
    low_mask = jnp.where(partners[0, 0] == half, partners[1, 0], partners[0, 0])
    masks = [2 ** (j + 1) - 1 for j in range(bits)]
    index = sum((low_mask >= m).astype(jnp.int32) for m in masks[1:])

    def fetch(j):
        return lambda k, v: exchange(
            fetch_kernel, 0, j, masks[j], shards, heads, [], (3 * tokens, width), k, v
        )

    def give_back(j):
        landing = pltpu.VMEM((3, rows, width * heads), jnp.bfloat16)
        return lambda k, v: exchange(
            return_kernel, bits, j, masks[j], shards, heads, [landing] * 2,
            (rows, width * heads), k, v
        )

    cand_keys, cand_values = lax.switch(index, [fetch(j) for j in range(bits)], keys, values)
    attended, grad_queries, key_terms, value_terms = attend(
        queries, d_out, cand_keys, cand_values
    )
    grad_keys, grad_values = lax.switch(
        index, [give_back(j) for j in range(bits)], key_terms, value_terms
    )
    return attended, grad_queries, grad_keys, grad_values


def solution(mesh):
    return jax.shard_map(
        body,
        mesh=mesh,
        in_specs=(
            P("ctx", "head"),
            P(("ctx", "head"), None),
            P(("ctx", "head"), None),
            P("ctx", "head"),
            P("ctx", None),
            P(),
        ),
        out_specs=(
            P("ctx", "head"),
            P("ctx", "head"),
            P(("ctx", "head"), None),
            P(("ctx", "head"), None),
        ),
        check_vma=False,
    )
```

```python
import functools

import jax
import jax.numpy as jnp
from jax import lax
from jax.experimental import pallas as pl
from jax.experimental.pallas import tpu as pltpu
from jax.sharding import PartitionSpec as P

HQ = 64
KVH = 4
DH = 128
BLK = 64
SEL = 12
PAIR = 2
SCALE = DH**-0.5
LOG2E = 1.4426950408889634
MESH = pl.DeviceIdType.MESH


def nt_dot(left, right):
    return lax.dot_general(
        left, right, (((1,), (1,)), ((), ())), preferred_element_type=jnp.float32
    )


def nn_dot(left, right):
    return jnp.dot(left, right, preferred_element_type=jnp.float32)


def one_head(q, g, k, v, kt, vt):
    qt = q.T
    gt = g.T
    scores = nn_dot(k, qt)
    grad_p = nn_dot(v, gt)
    top = jnp.max(scores, axis=0, keepdims=True)
    e = jnp.exp2((scores - top) * (SCALE * LOG2E))
    inv = 1.0 / jnp.sum(e, axis=0, keepdims=True)
    e_low = e.astype(jnp.bfloat16)
    ot = (nn_dot(vt, e_low) * inv).astype(jnp.bfloat16)
    gt32 = gt.astype(jnp.float32)
    delta = jnp.sum(gt32 * ot.astype(jnp.float32), axis=0, keepdims=True)
    ds = (e * (grad_p - delta)).astype(jnp.bfloat16)
    inv_s = inv * SCALE
    dqt = (nn_dot(kt, ds) * inv_s).astype(jnp.bfloat16)
    q_n = (qt.astype(jnp.float32) * inv_s).astype(jnp.bfloat16)
    g_n = (gt32 * inv).astype(jnp.bfloat16)
    return ot.T, dqt.T, ds, q_n, e_low, g_n


def partner_shards(low, shards):
    me = lax.axis_index("ctx")
    part = lax.rem(me, low + 1)
    return (me, me - part + (low - part), lax.rem(me + shards // 2, shards))


def peers(low, shards, heads):
    head = lax.axis_index("head")
    found = []
    for slot, shard in enumerate(partner_shards(low, shards)):
        for turn in range(heads):
            if slot or turn:
                found.append((slot, turn, shard, lax.rem(head + turn, heads)))
    return found


def greet(found):
    barrier = pltpu.get_barrier_semaphore()
    for slot, turn, shard, head in found:
        pl.semaphore_signal(barrier, inc=1, device_id=(shard, head), device_id_type=MESH)
    pl.semaphore_wait(barrier, len(found))


def aligned(start, size):
    return pl.ds(pl.multiple_of(start, size), size)


def fused_kernel(low, shards, heads, q_ref, g_ref, k_ref, v_ref, o_ref, dq_ref, gk_ref, gv_ref,
                 q_buf, g_buf, o_buf, dq_buf, kc, vc, kt_buf, vt_buf, ds_buf, e_buf, qn_buf, gn_buf,
                 kterm, vterm, kback, vback, in_sem, out_sem, own_sem, get_send, get_recv,
                 back_own, back_send, back_recv):
    me = lax.axis_index("head")
    rows = k_ref.shape[0]
    tokens, width = q_ref.shape
    groups = kc.shape[0]
    kv_width = groups * DH
    per_group = width // groups // DH
    found = peers(low, shards, heads)
    found = sorted(found, key=lambda f: -f[0])

    def columns(g):
        return pl.ds(g * per_group * DH, per_group * DH)

    loads = [
        [
            pltpu.make_async_copy(src.at[:, columns(g)], dst.at[:, columns(g)], in_sem.at[i, g])
            for i, (src, dst) in enumerate(((q_ref, q_buf), (g_ref, g_buf)))
        ]
        for g in range(groups)
    ]
    for load in loads[0]:
        load.start()
    greet(found)

    fetches = []
    for g in range(groups):
        copies = []
        for slot, turn, shard, head in found:
            for i, (src, dst) in enumerate(((k_ref, kc), (v_ref, vc))):
                copies.append(
                    pltpu.make_async_remote_copy(
                        src_ref=src.at[:, aligned(head * kv_width + g * DH, DH)],
                        dst_ref=dst.at[g, aligned(slot * rows * heads + me * rows, rows), :],
                        send_sem=get_send.at[i, g, slot, turn],
                        recv_sem=get_recv.at[i, g, slot, turn],
                        device_id=(shard, head),
                        device_id_type=MESH,
                    )
                )
        for i, (src, dst) in enumerate(((k_ref, kc), (v_ref, vc))):
            copies.append(
                pltpu.make_async_copy(
                    src.at[:, aligned(me * kv_width + g * DH, DH)],
                    dst.at[g, aligned(me * rows, rows), :],
                    own_sem.at[i, g],
                )
            )
        for copy in copies:
            copy.start()
        fetches.append(copies)
    for g in range(1, groups):
        for load in loads[g]:
            load.start()

    def give_back(g, slot):
        span = slice(slot * tokens, (slot + 1) * tokens)
        kterm[g, span, :] = nt_dot(ds_buf[g, span, :], qn_buf[g]).astype(jnp.bfloat16)
        vterm[g, span, :] = nt_dot(e_buf[g, span, :], gn_buf[g]).astype(jnp.bfloat16)
        copies = []
        for i, (src, dst) in enumerate(((kterm, kback), (vterm, vback))):
            place = aligned(me * kv_width + g * DH, DH)
            for where, turn, shard, head in found:
                if where == slot:
                    copies.append(
                        pltpu.make_async_remote_copy(
                            src_ref=src.at[g, aligned(slot * tokens + head * rows, rows), :],
                            dst_ref=dst.at[slot, :, place],
                            send_sem=back_send.at[i, g, slot, turn],
                            recv_sem=back_recv.at[i, g, slot, turn],
                            device_id=(shard, head),
                            device_id_type=MESH,
                        )
                    )
            if slot == 0:
                copies.append(
                    pltpu.make_async_copy(
                        src.at[g, aligned(me * rows, rows), :],
                        dst.at[0, :, place],
                        back_own.at[i, g],
                    )
                )
        for copy in copies:
            copy.start()
        return copies

    pending = []
    for g in range(groups):
        for load in loads[g]:
            load.wait()
        for copy in fetches[g]:
            copy.wait()
        kt_buf[...] = kc[g].T
        vt_buf[...] = vc[g].T

        def step(at, carry):
            k, v, kt, vt = kc[g], vc[g], kt_buf[...], vt_buf[...]
            for i in range(PAIR):
                head = at * PAIR + i
                cols = aligned((g * per_group + head) * DH, DH)
                lane = aligned(head * tokens, tokens)
                o, dq, ds, q_n, e_low, g_n = one_head(q_buf[:, cols], g_buf[:, cols], k, v, kt, vt)
                o_buf[:, cols] = o
                dq_buf[:, cols] = dq
                ds_buf[g, :, lane] = ds
                e_buf[g, :, lane] = e_low
                qn_buf[g, :, lane] = q_n
                gn_buf[g, :, lane] = g_n
            return carry

        lax.fori_loop(0, per_group // PAIR, step, 0)
        pending += give_back(g, 2)
        for i, (src, dst) in enumerate(((o_buf, o_ref), (dq_buf, dq_ref))):
            copy = pltpu.make_async_copy(
                src.at[:, columns(g)], dst.at[:, columns(g)], out_sem.at[i, g]
            )
            copy.start()
            pending.append(copy)
    for slot in (1, 0):
        for g in range(groups):
            pending += give_back(g, slot)
    for copy in pending:
        copy.wait()
    for out, got in ((gk_ref, kback), (gv_ref, vback)):
        total = got[0].astype(jnp.float32)
        for slot in (1, 2):
            total = total + got[slot].astype(jnp.float32)
        out[...] = total.astype(jnp.bfloat16)


def fused(index, low, shards, heads, queries, d_out, keys, values):
    tokens, width = queries.shape
    rows, kv_all = keys.shape
    groups = kv_all // heads // DH
    per_group = width // groups // DH
    cand = 3 * tokens
    elems = tokens * cand * per_group * groups
    anywhere = pl.BlockSpec(memory_space=pl.ANY)
    in_vmem = pl.BlockSpec(memory_space=pltpu.VMEM)
    low_type = jnp.bfloat16
    dma = pltpu.SemaphoreType.DMA
    return pl.pallas_call(
        functools.partial(fused_kernel, low, shards, heads),
        in_specs=[anywhere] * 4,
        out_specs=[anywhere, anywhere, in_vmem, in_vmem],
        out_shape=[jax.ShapeDtypeStruct(queries.shape, low_type)] * 2
        + [jax.ShapeDtypeStruct(keys.shape, low_type)] * 2,
        scratch_shapes=[pltpu.VMEM((tokens, width), low_type)] * 4
        + [pltpu.VMEM((groups, cand, DH), low_type)] * 2
        + [pltpu.VMEM((DH, cand), low_type)] * 2
        + [pltpu.VMEM((groups, cand, per_group * tokens), low_type)] * 2
        + [pltpu.VMEM((groups, DH, per_group * tokens), low_type)] * 2
        + [pltpu.VMEM((groups, cand, DH), low_type)] * 2
        + [pltpu.VMEM((3, rows, kv_all), low_type)] * 2
        + [dma((2, groups))] * 3
        + [dma((2, groups, 3, heads))] * 2
        + [dma((2, groups))]
        + [dma((2, groups, 3, heads))] * 2,
        compiler_params=pltpu.CompilerParams(
            collective_id=index, has_side_effects=True, vmem_limit_bytes=60 * 2**20
        ),
        cost_estimate=pl.CostEstimate(
            flops=12 * elems * DH, bytes_accessed=8 * tokens * width, transcendentals=elems
        ),
    )(queries, d_out, keys, values)


def body(queries, keys, values, d_out, selected, partners):
    shards = lax.axis_size("ctx")
    heads = lax.axis_size("head")
    bits = shards.bit_length() - 1
    tokens = queries.shape[0]
    assert selected.shape[1] == 3 * tokens // BLK
    half = shards // 2
    low_mask = jnp.where(partners[0, 0] == half, partners[1, 0], partners[0, 0])
    masks = [2 ** (j + 1) - 1 for j in range(bits)]
    index = sum((low_mask >= m).astype(jnp.int32) for m in masks[1:])

    branches = [functools.partial(fused, j, masks[j], shards, heads) for j in range(bits)]
    return lax.switch(index, branches, queries, d_out, keys, values)


def solution(mesh):
    return jax.shard_map(
        body,
        mesh=mesh,
        in_specs=(
            P("ctx", "head"),
            P(("ctx", "head"), None),
            P(("ctx", "head"), None),
            P("ctx", "head"),
            P("ctx", None),
            P(),
        ),
        out_specs=(
            P("ctx", "head"),
            P("ctx", "head"),
            P(("ctx", "head"), None),
            P(("ctx", "head"), None),
        ),
        check_vma=False,
    )
```

```python
import functools

import jax
import jax.numpy as jnp
from jax import lax
from jax.experimental import pallas as pl
from jax.experimental.pallas import tpu as pltpu
from jax.sharding import PartitionSpec as P

HQ = 64
KVH = 4
DH = 128
BLK = 64
SEL = 12
PAIR = 2
CHUNKS = 4
SCALE = DH**-0.5
LOG2E = 1.4426950408889634
MESH = pl.DeviceIdType.MESH


def nt_dot(left, right):
    return lax.dot_general(
        left, right, (((1,), (1,)), ((), ())), preferred_element_type=jnp.float32
    )


def nn_dot(left, right):
    return jnp.dot(left, right, preferred_element_type=jnp.float32)


def one_head(q, g, k, v, kt, vt):
    qt = q.T
    gt = g.T
    scores = nn_dot(k, qt)
    grad_p = nn_dot(v, gt)
    top = jnp.max(scores, axis=0, keepdims=True)
    e = jnp.exp2((scores - top) * (SCALE * LOG2E))
    inv = 1.0 / jnp.sum(e, axis=0, keepdims=True)
    e_low = e.astype(jnp.bfloat16)
    ot = (nn_dot(vt, e_low) * inv).astype(jnp.bfloat16)
    gt32 = gt.astype(jnp.float32)
    delta = jnp.sum(gt32 * ot.astype(jnp.float32), axis=0, keepdims=True)
    ds = (e * (grad_p - delta)).astype(jnp.bfloat16)
    inv_s = inv * SCALE
    dqt = (nn_dot(kt, ds) * inv_s).astype(jnp.bfloat16)
    q_n = (qt.astype(jnp.float32) * inv_s).astype(jnp.bfloat16)
    g_n = (gt32 * inv).astype(jnp.bfloat16)
    return ot.T, dqt.T, ds, q_n, e_low, g_n


def partner_shards(low, shards):
    me = lax.axis_index("ctx")
    part = lax.rem(me, low + 1)
    return (me, me - part + (low - part), lax.rem(me + shards // 2, shards))


def peers(low, shards, heads):
    head = lax.axis_index("head")
    found = []
    for slot, shard in enumerate(partner_shards(low, shards)):
        for turn in range(heads):
            if slot or turn:
                found.append((slot, turn, shard, lax.rem(head + turn, heads)))
    return found


def greet(found):
    barrier = pltpu.get_barrier_semaphore()
    for slot, turn, shard, head in found:
        pl.semaphore_signal(barrier, inc=1, device_id=(shard, head), device_id_type=MESH)
    pl.semaphore_wait(barrier, len(found))


def aligned(start, size):
    return pl.ds(pl.multiple_of(start, size), size)


def fused_kernel(low, shards, heads, q_ref, g_ref, k_ref, v_ref, o_ref, dq_ref, gk_ref, gv_ref,
                 q_buf, g_buf, o_buf, dq_buf, kc, vc, kt_buf, vt_buf, ds_buf, e_buf, qn_buf, gn_buf,
                 kterm, vterm, kback, vback, acc, in_sem, out_sem, own_sem, get_send, get_recv,
                 back_own, back_send, back_recv):
    me = lax.axis_index("head")
    rows = k_ref.shape[0]
    tokens, width = q_ref.shape
    groups = kc.shape[0]
    kv_width = groups * DH
    per_group = width // groups // DH
    found = peers(low, shards, heads)
    found = sorted(found, key=lambda f: -f[0])

    def columns(g):
        return aligned(g * per_group * DH, per_group * DH)

    def load(g):
        return [
            pltpu.make_async_copy(src.at[:, columns(g)], dst.at[:, columns(g)], in_sem.at[i, g])
            for i, (src, dst) in enumerate(((q_ref, q_buf), (g_ref, g_buf)))
        ]

    def fetch(g):
        copies = []
        for slot, turn, shard, head in found:
            for i, (src, dst) in enumerate(((k_ref, kc), (v_ref, vc))):
                copies.append(
                    pltpu.make_async_remote_copy(
                        src_ref=src.at[:, aligned(head * kv_width + g * DH, DH)],
                        dst_ref=dst.at[g, aligned(slot * rows * heads + me * rows, rows), :],
                        send_sem=get_send.at[i, g, slot, turn],
                        recv_sem=get_recv.at[i, g, slot, turn],
                        device_id=(shard, head),
                        device_id_type=MESH,
                    )
                )
        for i, (src, dst) in enumerate(((k_ref, kc), (v_ref, vc))):
            copies.append(
                pltpu.make_async_copy(
                    src.at[:, aligned(me * kv_width + g * DH, DH)],
                    dst.at[g, aligned(me * rows, rows), :],
                    own_sem.at[i, g],
                )
            )
        return copies

    def give_back(g, slot):
        copies = []
        for i, (src, dst) in enumerate(((kterm, kback), (vterm, vback))):
            place = aligned(me * kv_width + g * DH, DH)
            for where, turn, shard, head in found:
                if where == slot:
                    copies.append(
                        pltpu.make_async_remote_copy(
                            src_ref=src.at[g, aligned(slot * tokens + head * rows, rows), :],
                            dst_ref=dst.at[slot, :, place],
                            send_sem=back_send.at[i, g, slot, turn],
                            recv_sem=back_recv.at[i, g, slot, turn],
                            device_id=(shard, head),
                            device_id_type=MESH,
                        )
                    )
            if slot == 0:
                copies.append(
                    pltpu.make_async_copy(
                        src.at[g, aligned(me * rows, rows), :],
                        dst.at[0, :, place],
                        back_own.at[i, g],
                    )
                )
        return copies

    def write_out(g):
        return [
            pltpu.make_async_copy(src.at[:, columns(g)], dst.at[:, columns(g)], out_sem.at[i, g])
            for i, (src, dst) in enumerate(((o_buf, o_ref), (dq_buf, dq_ref)))
        ]

    def start(copies):
        for copy in copies:
            copy.start()

    def wait(copies):
        for copy in copies:
            copy.wait()

    def products(g, slot):
        span = slice(slot * tokens, (slot + 1) * tokens)
        chunk = tokens * per_group // CHUNKS

        def add(at, carry):
            lane = aligned(at * chunk, chunk)
            acc[0] += nt_dot(ds_buf[g, span, lane], qn_buf[g, :, lane])
            acc[1] += nt_dot(e_buf[g, span, lane], gn_buf[g, :, lane])
            return carry

        acc[...] = jnp.zeros_like(acc)
        lax.fori_loop(0, CHUNKS, add, 0)
        kterm[g, span, :] = acc[0].astype(jnp.bfloat16)
        vterm[g, span, :] = acc[1].astype(jnp.bfloat16)
        start(give_back(g, slot))

    greet(found)
    start(fetch(0))
    start(load(0))
    for g in range(1, groups):
        start(fetch(g))
        start(load(g))

    def one_group(g, carry):
        wait(load(g))
        wait(fetch(g))
        kt_buf[...] = kc[g].T
        vt_buf[...] = vc[g].T

        def step(at, carry):
            k, v, kt, vt = kc[g], vc[g], kt_buf[...], vt_buf[...]
            for i in range(PAIR):
                head = at * PAIR + i
                cols = aligned((g * per_group + head) * DH, DH)
                lane = aligned(head * tokens, tokens)
                o, dq, ds, q_n, e_low, g_n = one_head(q_buf[:, cols], g_buf[:, cols], k, v, kt, vt)
                o_buf[:, cols] = o
                dq_buf[:, cols] = dq
                ds_buf[g, :, lane] = ds
                e_buf[g, :, lane] = e_low
                qn_buf[g, :, lane] = q_n
                gn_buf[g, :, lane] = g_n
            return carry

        lax.fori_loop(0, per_group // PAIR, step, 0)
        products(g, 2)
        start(write_out(g))
        return carry

    lax.fori_loop(0, groups, one_group, 0)
    for slot in (1, 0):

        def one_slot(g, carry):
            products(g, slot)
            return carry

        lax.fori_loop(0, groups, one_slot, 0)

    def finish(g, carry):
        wait(write_out(g))
        for slot in (2, 1, 0):
            wait(give_back(g, slot))
        return carry

    lax.fori_loop(0, groups, finish, 0)
    for out, got in ((gk_ref, kback), (gv_ref, vback)):
        total = got[0].astype(jnp.float32)
        for slot in (1, 2):
            total = total + got[slot].astype(jnp.float32)
        out[...] = total.astype(jnp.bfloat16)


def fused(index, low, shards, heads, queries, d_out, keys, values):
    tokens, width = queries.shape
    rows, kv_all = keys.shape
    groups = kv_all // heads // DH
    per_group = width // groups // DH
    cand = 3 * tokens
    elems = tokens * cand * per_group * groups
    anywhere = pl.BlockSpec(memory_space=pltpu.HBM)
    in_vmem = pl.BlockSpec(memory_space=pltpu.VMEM)
    low_type = jnp.bfloat16
    dma = pltpu.SemaphoreType.DMA
    return pl.pallas_call(
        functools.partial(fused_kernel, low, shards, heads),
        in_specs=[anywhere] * 4,
        out_specs=[anywhere, anywhere, in_vmem, in_vmem],
        out_shape=[jax.ShapeDtypeStruct(queries.shape, low_type)] * 2
        + [jax.ShapeDtypeStruct(keys.shape, low_type)] * 2,
        scratch_shapes=[pltpu.VMEM((tokens, width), low_type)] * 4
        + [pltpu.VMEM((groups, cand, DH), low_type)] * 2
        + [pltpu.VMEM((DH, cand), low_type)] * 2
        + [pltpu.VMEM((groups, cand, per_group * tokens), low_type)] * 2
        + [pltpu.VMEM((groups, DH, per_group * tokens), low_type)] * 2
        + [pltpu.VMEM((groups, cand, DH), low_type)] * 2
        + [pltpu.VMEM((3, rows, kv_all), low_type)] * 2
        + [pltpu.VMEM((2, tokens, DH), jnp.float32)]
        + [dma((2, groups))] * 3
        + [dma((2, groups, 3, heads))] * 2
        + [dma((2, groups))]
        + [dma((2, groups, 3, heads))] * 2,
        compiler_params=pltpu.CompilerParams(
            collective_id=index, has_side_effects=True, vmem_limit_bytes=60 * 2**20
        ),
        cost_estimate=pl.CostEstimate(
            flops=12 * elems * DH, bytes_accessed=8 * tokens * width, transcendentals=elems
        ),
    )(queries, d_out, keys, values)


def body(queries, keys, values, d_out, selected, partners):
    shards = lax.axis_size("ctx")
    heads = lax.axis_size("head")
    bits = shards.bit_length() - 1
    tokens = queries.shape[0]
    assert selected.shape[1] == 3 * tokens // BLK
    half = shards // 2
    low_mask = jnp.where(partners[0, 0] == half, partners[1, 0], partners[0, 0])
    masks = [2 ** (j + 1) - 1 for j in range(bits)]
    index = sum((low_mask >= m).astype(jnp.int32) for m in masks[1:])

    branches = [functools.partial(fused, j, masks[j], shards, heads) for j in range(bits)]
    return lax.switch(index, branches, queries, d_out, keys, values)


def solution(mesh):
    return jax.shard_map(
        body,
        mesh=mesh,
        in_specs=(
            P("ctx", "head"),
            P(("ctx", "head"), None),
            P(("ctx", "head"), None),
            P("ctx", "head"),
            P("ctx", None),
            P(),
        ),
        out_specs=(
            P("ctx", "head"),
            P("ctx", "head"),
            P(("ctx", "head"), None),
            P(("ctx", "head"), None),
        ),
        check_vma=False,
    )
```

```python
import functools

import jax
import jax.numpy as jnp
from jax import lax
from jax.experimental import pallas as pl
from jax.experimental.pallas import tpu as pltpu
from jax.sharding import PartitionSpec as P

HQ = 64
KVH = 4
DH = 128
BLK = 64
SEL = 12
PAIR = 4
CHUNKS = 8
SCALE = DH**-0.5
LOG2E = 1.4426950408889634
MESH = pl.DeviceIdType.MESH


def nt_dot(left, right):
    return lax.dot_general(
        left, right, (((1,), (1,)), ((), ())), preferred_element_type=jnp.float32
    )


def nn_dot(left, right):
    return jnp.dot(left, right, preferred_element_type=jnp.float32)


def one_head(qt, gt, k, v, kt, vt):
    scores = nn_dot(k, qt)
    grad_p = nn_dot(v, gt)
    top = jnp.max(scores, axis=0, keepdims=True)
    e = jnp.exp2((scores - top) * (SCALE * LOG2E))
    inv = 1.0 / jnp.sum(e, axis=0, keepdims=True)
    e_low = e.astype(jnp.bfloat16)
    ot = (nn_dot(vt, e_low) * inv).astype(jnp.bfloat16)
    gt32 = gt.astype(jnp.float32)
    delta = jnp.sum(gt32 * ot.astype(jnp.float32), axis=0, keepdims=True)
    ds = (e * (grad_p - delta)).astype(jnp.bfloat16)
    inv_s = inv * SCALE
    dqt = (nn_dot(kt, ds) * inv_s).astype(jnp.bfloat16)
    q_n = (qt.astype(jnp.float32) * inv_s).astype(jnp.bfloat16)
    g_n = (gt32 * inv).astype(jnp.bfloat16)
    return ot.T, dqt.T, ds, q_n, e_low, g_n


def partner_shards(low, shards):
    me = lax.axis_index("ctx")
    part = lax.rem(me, low + 1)
    return (me, me - part + (low - part), lax.rem(me + shards // 2, shards))


def peers(low, shards, heads):
    head = lax.axis_index("head")
    found = []
    for slot, shard in enumerate(partner_shards(low, shards)):
        for turn in range(heads):
            if slot or turn:
                found.append((slot, turn, shard, lax.rem(head + turn, heads)))
    return found


def greet(found):
    barrier = pltpu.get_barrier_semaphore()
    for slot, turn, shard, head in found:
        pl.semaphore_signal(barrier, inc=1, device_id=(shard, head), device_id_type=MESH)
    pl.semaphore_wait(barrier, len(found))


def aligned(start, size):
    return pl.ds(pl.multiple_of(start, size), size)


def fused_kernel(low, shards, heads, q_ref, g_ref, k_ref, v_ref, o_ref, dq_ref, gk_ref, gv_ref,
                 q_buf, g_buf, o_buf, dq_buf, kc, vc, kt_buf, vt_buf, ds_buf, e_buf, qn_buf, gn_buf,
                 kterm, vterm, kback, vback, acc, qt_buf, gt_buf, in_sem, out_sem, own_sem, get_send, get_recv,
                 back_own, back_send, back_recv):
    me = lax.axis_index("head")
    rows = k_ref.shape[0]
    tokens, width = q_ref.shape
    groups = kc.shape[0]
    kv_width = groups * DH
    per_group = width // groups // DH
    found = peers(low, shards, heads)
    found = sorted(found, key=lambda f: -f[0])

    def columns(g):
        return aligned(g * per_group * DH, per_group * DH)

    def load(g):
        return [
            pltpu.make_async_copy(src.at[:, columns(g)], dst.at[:, columns(g)], in_sem.at[i, g])
            for i, (src, dst) in enumerate(((q_ref, q_buf), (g_ref, g_buf)))
        ]

    def fetch(g):
        copies = []
        for slot, turn, shard, head in found:
            for i, (src, dst) in enumerate(((k_ref, kc), (v_ref, vc))):
                copies.append(
                    pltpu.make_async_remote_copy(
                        src_ref=src.at[:, aligned(head * kv_width + g * DH, DH)],
                        dst_ref=dst.at[g, aligned(slot * rows * heads + me * rows, rows), :],
                        send_sem=get_send.at[i, g, slot, turn],
                        recv_sem=get_recv.at[i, g, slot, turn],
                        device_id=(shard, head),
                        device_id_type=MESH,
                    )
                )
        for i, (src, dst) in enumerate(((k_ref, kc), (v_ref, vc))):
            copies.append(
                pltpu.make_async_copy(
                    src.at[:, aligned(me * kv_width + g * DH, DH)],
                    dst.at[g, aligned(me * rows, rows), :],
                    own_sem.at[i, g],
                )
            )
        return copies

    def give_back(g, slot):
        copies = []
        for i, (src, dst) in enumerate(((kterm, kback), (vterm, vback))):
            place = aligned(me * kv_width + g * DH, DH)
            for where, turn, shard, head in found:
                if where == slot:
                    copies.append(
                        pltpu.make_async_remote_copy(
                            src_ref=src.at[g, aligned(slot * tokens + head * rows, rows), :],
                            dst_ref=dst.at[slot, :, place],
                            send_sem=back_send.at[i, g, slot, turn],
                            recv_sem=back_recv.at[i, g, slot, turn],
                            device_id=(shard, head),
                            device_id_type=MESH,
                        )
                    )
            if slot == 0:
                copies.append(
                    pltpu.make_async_copy(
                        src.at[g, aligned(me * rows, rows), :],
                        dst.at[0, :, place],
                        back_own.at[i, g],
                    )
                )
        return copies

    def write_out(g):
        return [
            pltpu.make_async_copy(src.at[:, columns(g)], dst.at[:, columns(g)], out_sem.at[i, g])
            for i, (src, dst) in enumerate(((o_buf, o_ref), (dq_buf, dq_ref)))
        ]

    def start(copies):
        for copy in copies:
            copy.start()

    def wait(copies):
        for copy in copies:
            copy.wait()

    def products(g, slot):
        span = slice(slot * tokens, (slot + 1) * tokens)
        chunk = tokens * per_group // CHUNKS

        def add(at, carry):
            lane = aligned(at * chunk, chunk)
            acc[0] += nt_dot(ds_buf[g, span, lane], qn_buf[g, :, lane])
            acc[1] += nt_dot(e_buf[g, span, lane], gn_buf[g, :, lane])
            return carry

        acc[...] = jnp.zeros_like(acc)
        lax.fori_loop(0, CHUNKS, add, 0)
        kterm[g, span, :] = acc[0].astype(jnp.bfloat16)
        vterm[g, span, :] = acc[1].astype(jnp.bfloat16)
        start(give_back(g, slot))

    for g in range(groups):
        start(load(g))
    greet(found)
    start(fetch(0))

    def turn_group(g, carry):
        wait(load(g))

        def turn_head(head, inner):
            at = aligned(head * DH, DH)
            lane = aligned(head * tokens, tokens)
            qt_buf[:, lane] = q_buf[:, at].T
            gt_buf[:, lane] = g_buf[:, at].T
            return inner

        return lax.fori_loop(g * per_group, (g + 1) * per_group, turn_head, carry)

    lax.fori_loop(0, groups, turn_group, 0)

    def one_group(g, carry):
        wait(fetch(g))

        @pl.when(g + 1 < groups)
        def _():
            start(fetch(g + 1))

        kt_buf[...] = kc[g].T
        vt_buf[...] = vc[g].T

        def step(at, carry):
            k, v, kt, vt = kc[g], vc[g], kt_buf[...], vt_buf[...]
            for i in range(PAIR):
                head = at * PAIR + i
                cols = aligned((g * per_group + head) * DH, DH)
                lane = aligned(head * tokens, tokens)
                turned = aligned((g * per_group + head) * tokens, tokens)
                o, dq, ds, q_n, e_low, g_n = one_head(
                    qt_buf[:, turned], gt_buf[:, turned], k, v, kt, vt
                )
                o_buf[:, cols] = o
                dq_buf[:, cols] = dq
                ds_buf[g, :, lane] = ds
                e_buf[g, :, lane] = e_low
                qn_buf[g, :, lane] = q_n
                gn_buf[g, :, lane] = g_n
            return carry

        lax.fori_loop(0, per_group // PAIR, step, 0)
        products(g, 2)
        start(write_out(g))
        return carry

    lax.fori_loop(0, groups, one_group, 0)
    for slot in (1, 0):

        def one_slot(g, carry):
            products(g, slot)
            return carry

        lax.fori_loop(0, groups, one_slot, 0)

    def finish(g, carry):
        wait(write_out(g))
        for slot in (2, 1, 0):
            wait(give_back(g, slot))
        return carry

    lax.fori_loop(0, groups, finish, 0)
    for out, got in ((gk_ref, kback), (gv_ref, vback)):
        total = got[0].astype(jnp.float32)
        for slot in (1, 2):
            total = total + got[slot].astype(jnp.float32)
        out[...] = total.astype(jnp.bfloat16)


def fused(index, low, shards, heads, queries, d_out, keys, values):
    tokens, width = queries.shape
    rows, kv_all = keys.shape
    groups = kv_all // heads // DH
    per_group = width // groups // DH
    cand = 3 * tokens
    elems = tokens * cand * per_group * groups
    anywhere = pl.BlockSpec(memory_space=pltpu.HBM)
    in_vmem = pl.BlockSpec(memory_space=pltpu.VMEM)
    low_type = jnp.bfloat16
    dma = pltpu.SemaphoreType.DMA
    return pl.pallas_call(
        functools.partial(fused_kernel, low, shards, heads),
        in_specs=[anywhere] * 4,
        out_specs=[anywhere, anywhere, in_vmem, in_vmem],
        out_shape=[jax.ShapeDtypeStruct(queries.shape, low_type)] * 2
        + [jax.ShapeDtypeStruct(keys.shape, low_type)] * 2,
        scratch_shapes=[pltpu.VMEM((tokens, width), low_type)] * 4
        + [pltpu.VMEM((groups, cand, DH), low_type)] * 2
        + [pltpu.VMEM((DH, cand), low_type)] * 2
        + [pltpu.VMEM((groups, cand, per_group * tokens), low_type)] * 2
        + [pltpu.VMEM((groups, DH, per_group * tokens), low_type)] * 2
        + [pltpu.VMEM((groups, cand, DH), low_type)] * 2
        + [pltpu.VMEM((3, rows, kv_all), low_type)] * 2
        + [pltpu.VMEM((2, tokens, DH), jnp.float32)]
        + [pltpu.VMEM((DH, width // DH * tokens), low_type)] * 2
        + [dma((2, groups))] * 3
        + [dma((2, groups, 3, heads))] * 2
        + [dma((2, groups))]
        + [dma((2, groups, 3, heads))] * 2,
        compiler_params=pltpu.CompilerParams(
            collective_id=index, has_side_effects=True, vmem_limit_bytes=60 * 2**20
        ),
        cost_estimate=pl.CostEstimate(
            flops=12 * elems * DH, bytes_accessed=8 * tokens * width, transcendentals=elems
        ),
    )(queries, d_out, keys, values)


def body(queries, keys, values, d_out, selected, partners):
    shards = lax.axis_size("ctx")
    heads = lax.axis_size("head")
    bits = shards.bit_length() - 1
    tokens = queries.shape[0]
    assert selected.shape[1] == 3 * tokens // BLK
    half = shards // 2
    low_mask = jnp.where(partners[0, 0] == half, partners[1, 0], partners[0, 0])
    masks = [2 ** (j + 1) - 1 for j in range(bits)]
    index = sum((low_mask >= m).astype(jnp.int32) for m in masks[1:])

    branches = [functools.partial(fused, j, masks[j], shards, heads) for j in range(bits)]
    return lax.switch(index, branches, queries, d_out, keys, values)


def solution(mesh):
    return jax.shard_map(
        body,
        mesh=mesh,
        in_specs=(
            P("ctx", "head"),
            P(("ctx", "head"), None),
            P(("ctx", "head"), None),
            P("ctx", "head"),
            P("ctx", None),
            P(),
        ),
        out_specs=(
            P("ctx", "head"),
            P("ctx", "head"),
            P(("ctx", "head"), None),
            P(("ctx", "head"), None),
        ),
        check_vma=False,
    )
```
